32 devices in a mesh: dp: 16 (over z, x, core), expert: 2 (over y).
Axes of the slice: x: 2, y: 2, z: 4, core: 2. Of those that a mesh axis runs over, the one named last changes fastest.
Arguments:
- tokens: bfloat16 [2048, 4096], P('dp', 'expert'), may hold values from -6 to 6
- expert_ids: int32 [2048, 8], P('dp'), may hold values from 0 to 31, all different within a row; in each aligned block of 128 rows (0 to 127, 128 to 255, ...) at most 48 rows name the same one
- gate_prob: float32 [2048, 8], P('dp'), may hold values from 0.05 to 1
- w_gate: bfloat16 [32, 1536, 4096], P('dp', 'expert'), may hold values from -0.09375 to 0.09375
- w_up: bfloat16 [32, 1536, 4096], P('dp', 'expert'), may hold values from -0.09375 to 0.09375
- w_down: bfloat16 [32, 1536, 4096], P('dp', 'expert'), may hold values from -0.21875 to 0.21875
Outputs:
- mixed: bfloat16 [2048, 4096], P('dp', 'expert')
The draws below stay inside these ranges and needn't reach their ends.
Inputs may be any that keep to these rules, and one draw needn't show every extreme that they name: `expert_ids`: within the 128 tokens of one index of dp no expert is named more than 48 times, a bound that some block reaches; a token's 8 experts differ.
All inputs are finite; a program needn't handle non-finite values.
Results may differ from the reference program's by a relative error of at most 0.014.
Values may be sent and summed in bfloat16 or wider, within the bound.
No kernel may reach another device: no remote copies, remote signals or barrier semaphores. Data moves between devices by JAX's collectives and lax.ppermute only.
A program may use at most 128 MiB of HBM per device.

```python
import math
import jax
import jax.numpy as jnp
import numpy as np
from jax import lax

D = 4096
FF = 1536
TOP = 8
TOK_DEV = 128
EXPERTS = 32
CAP = 48
TOKENS = 2048
N_EXPERT = 2


def strengthened(entries, rng, source, target, parts, factor):
    def block_of(axis_at):
        return (jnp.arange(entries.shape[axis_at]) // (entries.shape[axis_at] // parts)).reshape((-1,) + (1,) * (entries.ndim - 1 - axis_at))

    one_side = jax.random.permutation(rng, parts)[block_of(target)]
    far = (block_of(target) + parts // 2) % parts
    return jnp.where((block_of(source) == one_side) | (block_of(source) == far), factor * entries, entries)


def block_levels(key, shape, shards, smallest, high):
    gain, own = 1.0, jax.random.fold_in(key, 6)
    for axis_at, blocks in shards:
        heights = jnp.exp(jax.random.uniform(jax.random.fold_in(own, axis_at), (blocks,), jnp.float32, smallest / len(shards), high / len(shards)))
        gain = gain * jnp.repeat(heights, shape[axis_at] // blocks).reshape([-1 if axis == axis_at else 1 for axis in range(len(shape))])
    return gain


def routed_block(stream_key, own, number, rows, count, top, reach, lean):
    order = jax.random.permutation(stream_key, count)
    packed, ordinary = shares(count, rows * top, reach, lean, True), shares(count, rows * top, reach, lean, False)
    places = jnp.arange(count)

    def named(lengths, offset_by):
        used = int((lengths > 0).sum())
        fixed = max(1, used // 4)
        moved = fixed + (places - fixed + offset_by * (used - fixed)) % max(1, count - fixed)
        return jnp.zeros((count,), jnp.int32).at[order[jnp.where(places < fixed, places, moved)]].set(jnp.asarray(lengths, jnp.int32))

    lengths = jnp.where(number % 4 == 0, named(packed, number // 4), named(ordinary, number - number // 4 - 1))
    mixed = jax.random.permutation(jax.random.fold_in(own, 3), count)
    donor, receiver = mixed[0:count // 2 * 2:2], mixed[1:count // 2 * 2:2]
    room = jnp.minimum(lengths[donor] - 1, reach - lengths[receiver]) // 2
    room = jnp.where((donor == order[0]) | (receiver == order[0]) | (lengths[receiver] == 0), 0, jnp.maximum(room, 0))
    moved = jax.random.randint(jax.random.fold_in(own, 4), (count // 2,), 0, 1 << 20) % (room + 1)
    lengths = lengths.at[donor].add(-moved).at[receiver].add(moved)
    members = jnp.searchsorted(jnp.cumsum(lengths), jnp.arange(rows * top), side="right").astype(jnp.int32)
    table = members.reshape(top, rows).T
    table = table[jax.random.permutation(jax.random.fold_in(own, 1), rows)]
    offset_by = jax.random.randint(jax.random.fold_in(own, 2), (rows, 1), 0, top)
    return jnp.take_along_axis(table, (jnp.arange(top)[None, :] + offset_by) % top, axis=1)


def shares(count, total, most, lean, full):
    loads = [(1 << 20) // math.isqrt(grade ** lean) + 1 for grade in range(1, count + 1)]
    largest = most if full else min(most, max(-(-total // count), total * loads[0] // sum(loads)))
    least = 1 if total - largest >= count - 1 else 0
    counts, spare = [largest] + [least] * (count - 1), total - largest - least * (count - 1)
    while spare > 0:
        movable = [i for i in range(1, count) if counts[i] < largest] or [i for i in range(1, count) if counts[i] < most]
        mass, remaining = sum([loads[i] for i in movable]), spare
        for i in movable:
            more = min(most - counts[i], max(1, remaining * loads[i] // mass), spare)
            counts[i] = counts[i] + more
            spare = spare - more
    return np.array(counts)


def normal_values(stream_key, shape, scale, limit, shards=(), kind=jnp.bfloat16):
    drawn = scale * jax.random.normal(stream_key, shape, jnp.float32)
    if shards:
        drawn = drawn * block_levels(stream_key, shape, shards, -0.22, 0.18)
    return jnp.clip(drawn, -limit, limit).astype(kind)


def bell_draw_with(rng, dims, width, reach, shards, heavy, held_as=jnp.bfloat16):
    values = width * jax.random.normal(rng, dims, jnp.float32)
    if shards:
        values = values * block_levels(rng, dims, shards, -0.22, 0.18)
    return jnp.clip(strengthened(values, jax.random.fold_in(rng, 3), *heavy), -reach, reach).astype(held_as)


def setup_inputs(seed: int = 0) -> dict:
    splits = jax.random.split(jax.random.key(seed), 7)
    tokens = normal_values(splits[0], (TOKENS, D), 1.0, 6.0, ((0, 16), (1, 2)))
    expert_ids_keys = jax.random.split(jax.random.fold_in(splits[1], 1), TOKENS // TOK_DEV)
    expert_ids_turns = jax.random.permutation(jax.random.fold_in(splits[1], 3), TOKENS // TOK_DEV)
    expert_ids = jax.vmap(lambda own, number: routed_block(jax.random.fold_in(splits[1], 2), own, number, TOK_DEV, EXPERTS, TOP, CAP, 2))(expert_ids_keys, expert_ids_turns).reshape((TOKENS, TOP))
    gate_prob = jnp.clip(jnp.exp(math.log(1.0) - 2.9957323 * jax.random.uniform(splits[2], (TOKENS, TOP), jnp.float32) ** block_levels(splits[2], (TOKENS, TOP), ((0, 16),), -0.2, 0.2)), 0.05, 1.0)
    w_gate = normal_values(splits[3], (EXPERTS, FF, D), D ** -0.5, 0.09375, ((0, 16), (1, 2)))
    w_up = normal_values(splits[4], (EXPERTS, FF, D), D ** -0.5, 0.09375, ((0, 16), (1, 2)))
    w_down = bell_draw_with(splits[5], (EXPERTS, FF, D), FF ** -0.5, 0.21875, ((0, 16), (1, 2)), (1, 2, 2, 2.0))
    return {"tokens": tokens, "expert_ids": expert_ids, "gate_prob": gate_prob, "w_gate": w_gate, "w_up": w_up, "w_down": w_down}


def reference(tokens, expert_ids, gate_prob, w_gate, w_up, w_down):
    token_count = tokens.shape[0]
    blocks = token_count // TOK_DEV
    pairs = TOK_DEV * TOP
    block_ids = expert_ids.reshape(blocks, pairs).astype(jnp.int32)
    onehot = (block_ids[:, :, None] == jnp.arange(EXPERTS, dtype=jnp.int32)[None, None, :]).astype(jnp.int32)
    before = jnp.cumsum(onehot, axis=1, dtype=jnp.int32) - onehot
    slot_pos = jnp.sum(before * onehot, axis=2, dtype=jnp.int32)
    block_of = jnp.broadcast_to(jnp.arange(blocks, dtype=jnp.int32)[:, None], (blocks, pairs))
    token_of = block_of * TOK_DEV + (jnp.arange(pairs, dtype=jnp.int32) // TOP)[None, :]
    slot_table = jnp.full((EXPERTS, blocks, CAP), token_count, jnp.int32).at[block_ids, block_of, slot_pos].set(token_of)
    slot_weight = jnp.zeros((EXPERTS, blocks, CAP), jnp.float32).at[block_ids, block_of, slot_pos].set(gate_prob.reshape(blocks, pairs).astype(jnp.float32))
    padded = jnp.concatenate([tokens, jnp.zeros((1, tokens.shape[1]), tokens.dtype)], axis=0)
    group = FF // N_EXPERT

    def expert_step(accum, inputs):
        table, weight, gate_w, up_w, down_w = inputs
        index_rows = table.reshape(-1)
        routed = padded[index_rows]
        gate_sum = jnp.dot(routed, gate_w.T, preferred_element_type=jnp.float32)
        up_sum = jnp.dot(routed, up_w.T, preferred_element_type=jnp.float32)
        hidden = (jax.nn.silu(gate_sum) * up_sum).astype(jnp.bfloat16)
        expert_out = jnp.zeros((routed.shape[0], tokens.shape[1]), jnp.float32)
        for shard in range(N_EXPERT):
            partial_value = jnp.dot(hidden[:, shard * group:(shard + 1) * group], down_w[shard * group:(shard + 1) * group], preferred_element_type=jnp.float32)
            partial_value = lax.optimization_barrier(partial_value.astype(jnp.bfloat16))
            expert_out = expert_out + partial_value.astype(jnp.float32)
        accum = accum.at[index_rows].add(weight.reshape(-1)[:, None] * expert_out)
        return accum, None

    start_accum = jnp.zeros((token_count + 1, tokens.shape[1]), jnp.float32)
    accum, _ = lax.scan(expert_step, start_accum, (slot_table, slot_weight, w_gate, w_up, w_down))
    return accum[:token_count].astype(jnp.bfloat16)
```

```python
import functools

import jax
import jax.numpy as jnp
from jax import lax
from jax.experimental import pallas as pl
from jax.experimental.pallas import tpu as pltpu
from jax.sharding import PartitionSpec as P

TOP = 8
AXES = ("dp", "expert")
F32, BF16 = jnp.float32, jnp.bfloat16

BIT = {"Z": 8, "z": 4, "a": 2, "b": 1}
HOP = {8: "Z", 4: "z", 12: "z", 2: "a", 10: "a", 6: "a", 14: "a", 1: "b", 9: "b", 5: "b", 13: "b", 3: "b", 11: "b", 7: "z", 15: "z"}
SPREAD = (8, 4, 1, 2, 3, 5, 6, 9, 10, 12, 11, 7, 13, 14, 15)


def link_pairs(link):
    pairs = []
    for here in range(32):
        along_x, along_y = 4, 1
        first = (here >> 1) & 1 == 0
        step = {"Z": 16, "z": 8, "core": 2, "a": along_x if first else along_y, "b": along_y if first else along_x}[link]
        pairs.append((here, here ^ step))
    return pairs


def hop(value, link):
    return lax.ppermute(value, AXES, link_pairs(link))


def silu(v):
    return v / (1.0 + jnp.exp(-v))


def experts_kernel(slots, hid_steps, place, *refs):
    (pieces, (pos, weight, w_gate, w_up, w_down, mine, other, routed, hidden, pick, put, scale)) = refs[:8], refs[8:]
    step = pl.program_id(0)
    core, side = place[0], place[1]
    experts = w_down.shape[0]
    rows, half = pieces[0].shape
    used = 4 * slots
    hid_block = w_gate.shape[1]
    per_expert = hid_steps // experts

    @pl.when(step == 0)
    def _():
        for block in range(4):
            for e in range(experts):
                line = block * experts + e
                at = pl.ds(e * slots, slots)
                slot = lax.broadcasted_iota(jnp.int32, (slots, rows), 0).astype(F32)
                chosen = jnp.where(slot == pos[line : line + 1, :], 1.0, 0.0)
                pick[block, at, :] = chosen.astype(BF16)
                scale[e, pl.ds(block * slots, slots), :] = jnp.sum(chosen * weight[line : line + 1, :], axis=1, keepdims=True)
            put[block] = pick[block].astype(F32).T.astype(BF16)
        for number, piece in enumerate(pieces):
            own = number < 4
            a, b = (number % 4) // 2, number % 2
            first = (core == 0) if own else (core == 1)
            x, y = jnp.where(first, a, b), jnp.where(first, b, a)
            block = x + (0 if own else 2)
            column = (y ^ side) * half
            chosen = pick[block]
            row = pl.multiple_of(block * slots, 16)
            for part in range(4):
                width = half // 4
                got = jnp.dot(chosen, piece[:, part * width : (part + 1) * width], preferred_element_type=F32).astype(BF16)
                to = pl.ds(pl.multiple_of(column + part * width, width), width)
                for e in range(experts):
                    routed[e, pl.ds(row, slots), to] = got[e * slots : (e + 1) * slots]

    @pl.when(step < hid_steps)
    def _():
        e = step // per_expert
        at = pl.multiple_of((step % per_expert) * hid_block, hid_block)
        contract = (((1,), (1,)), ((), ()))
        rows_in = routed[e]
        gate = lax.dot_general(rows_in, w_gate[0], contract, preferred_element_type=F32)
        up = lax.dot_general(rows_in, w_up[0], contract, preferred_element_type=F32)
        hidden[e, :, pl.ds(at, hid_block)] = (silu(gate) * up).astype(BF16)

    @pl.when(step >= hid_steps)
    def _():
        outs = []
        for e in range(experts):
            part = jnp.dot(hidden[e], w_down[e], preferred_element_type=F32)
            outs.append((part * scale[e]).astype(BF16))
        for block in range(4):
            these = jnp.concatenate([o[block * slots : (block + 1) * slots] for o in outs], axis=0)
            total = jnp.dot(put[block], these, preferred_element_type=F32).astype(BF16)
            if block < 2:
                mine[block, 0] = total
            else:
                other[block - 2, 0] = total


def run_experts(place, pieces, pos, weight, w_gate, w_up, w_down, slots):
    experts, hid, width = w_gate.shape
    rows, half = pieces[0].shape
    hid_block, col_block = 256, 512
    per_expert = hid // hid_block
    hid_steps, col_steps = experts * per_expert, width // col_block
    half_steps = half // col_block
    whole = pl.BlockSpec((rows, half), lambda s, place: (0, 0))
    small = pl.BlockSpec((4 * experts, rows), lambda s, place: (0, 0))

    def hid_at(s, place):
        t = jnp.minimum(s, hid_steps - 1)
        return t // per_expert, t % per_expert, 0

    def col_at(s, place):
        return 0, 0, jnp.maximum(s - hid_steps, 0)

    def out_at(s, place):
        t = jnp.maximum(s - hid_steps, 0)
        return 0, (t // half_steps) ^ place[1], 0, t % half_steps

    used = 4 * slots
    out = jax.ShapeDtypeStruct((2, 2, rows, half), BF16)
    return pl.pallas_call(
        functools.partial(experts_kernel, slots, hid_steps),
        out_shape=(out, out),
        grid_spec=pltpu.PrefetchScalarGridSpec(
            num_scalar_prefetch=1,
            grid=(hid_steps + col_steps,),
            in_specs=[whole] * 8
            + [small, small]
            + [pl.BlockSpec((1, hid_block, width), hid_at)] * 2
            + [pl.BlockSpec((experts, hid, col_block), col_at)],
            out_specs=[pl.BlockSpec((2, 1, rows, col_block), out_at)] * 2,
            scratch_shapes=[
                pltpu.VMEM((experts, used, width), BF16),
                pltpu.VMEM((experts, used, hid), BF16),
                pltpu.VMEM((4, experts * slots, rows), BF16),
                pltpu.VMEM((4, rows, experts * slots), BF16),
                pltpu.VMEM((experts, used, 1), F32),
            ],
        ),
        compiler_params=pltpu.CompilerParams(vmem_limit_bytes=40 << 20),
        cost_estimate=pl.CostEstimate(
            flops=6 * experts * used * hid * width,
            bytes_accessed=6 * experts * hid * width + 32 * rows * half,
            transcendentals=experts * used * hid,
        ),
        name="experts",
    )(place, *pieces, pos, weight, w_gate, w_up, w_down)


def slot_tables(expert_ids, gate_prob, experts_all):
    named = expert_ids[:, :, None] == jnp.arange(experts_all, dtype=jnp.int32)[None, None, :]
    chosen = jnp.any(named, axis=1)
    weight = jnp.sum(jnp.where(named, gate_prob[:, :, None], 0.0), axis=1)
    rows = expert_ids.shape[0]
    earlier = jnp.tril(jnp.ones((rows, rows), BF16), -1)
    before = jnp.dot(earlier, chosen.astype(BF16), preferred_element_type=F32)
    slot = jnp.where(chosen, before, -1.0)
    return jnp.stack([slot.T, weight.T], axis=1)


def on_block(tokens, expert_ids, gate_prob, w_gate, w_up, w_down):
    dp_count, me = lax.axis_size("dp"), lax.axis_index("dp")
    rows, half = tokens.shape
    experts = w_gate.shape[0]
    experts_all = experts * dp_count
    capacity = 3 * rows * TOP // (2 * experts_all)
    slots = -(-capacity // 16) * 16
    core = me % 2
    place = jnp.stack([core, lax.axis_index("expert")]).astype(jnp.int32)

    tables = slot_tables(expert_ids, gate_prob, experts_all)
    tables = lax.all_to_all(
        tables.reshape(dp_count, experts, 2, rows), "dp", split_axis=0, concat_axis=0, tiled=True
    )
    tables = tables[me ^ jnp.arange(dp_count, dtype=jnp.int32)]

    held = {0: tokens}
    for j in SPREAD:
        held[j] = hop(held[j & ~BIT[HOP[j]]], HOP[j])
    across = {j: hop(held[j], "core") for j in (0, *SPREAD)}

    sums = {}
    for group in (0, 4, 8, 12):
        order = [group | b for b in (0, 2, 1, 3)]
        chosen = jnp.stack([tables[r] for r in order])
        pos = chosen[:, :, 0].reshape(4 * experts, rows)
        weight = chosen[:, :, 1].reshape(4 * experts, rows)
        pieces = [held[group | q] for q in range(4)] + [across[group | q] for q in range(4)]
        mine, other = run_experts(place, pieces, pos, weight, w_gate, w_up, w_down, slots)
        back = hop(other, "core")
        mine, back = (v.reshape(4, rows, half) for v in (mine, back))
        for q in range(4):
            at = jnp.where(core == 0, q, (q % 2) * 2 + q // 2)
            sums[group | q] = [lax.dynamic_index_in_dim(v, at, 0, keepdims=False) for v in (mine, back)]

    def total(j):
        terms = sums[j] + [hop(total(k), HOP[k]) for k in SPREAD if k & ~BIT[HOP[k]] == j]
        return sum(t.astype(F32) for t in terms).astype(BF16)

    return total(0)


def on_device(tokens, expert_ids, gate_prob, w_gate, w_up, w_down):
    dp_count = lax.axis_size("dp")
    tok_rows = tokens.shape[0]
    local_experts = w_gate.shape[0]
    experts_all = local_experts * dp_count
    capacity = 3 * tok_rows * TOP // (2 * experts_all)
    flat_ids = expert_ids.reshape(-1)
    pair_count = flat_ids.shape[0]
    onehot = (flat_ids[:, None] == jnp.arange(experts_all, dtype=jnp.int32)[None, :]).astype(
        jnp.int32
    )
    before = jnp.cumsum(onehot, axis=0, dtype=jnp.int32) - onehot
    slot_pos = jnp.sum(before * onehot, axis=1, dtype=jnp.int32)
    flat_slot = flat_ids * capacity + slot_pos
    owner_row = jnp.arange(pair_count, dtype=jnp.int32) // TOP
    source_row = (
        jnp.full((experts_all * capacity,), tok_rows, jnp.int32).at[flat_slot].set(owner_row)
    )
    weights = gate_prob.reshape(-1)
    gathered = lax.all_gather(tokens, "expert", axis=1, tiled=True)
    padded = jnp.concatenate([gathered, jnp.zeros((1, gathered.shape[1]), gathered.dtype)], axis=0)
    arrived = lax.all_to_all(
        padded[source_row].reshape(dp_count, local_experts, capacity, gathered.shape[1]),
        "dp",
        split_axis=0,
        concat_axis=0,
        tiled=True,
    )
    gate_sum = jnp.einsum("sqcd,qfd->sqcf", arrived, w_gate, preferred_element_type=jnp.float32)
    up_sum = jnp.einsum("sqcd,qfd->sqcf", arrived, w_up, preferred_element_type=jnp.float32)
    hidden = (jax.nn.silu(gate_sum) * up_sum).astype(jnp.bfloat16)
    partial_value = jnp.einsum("sqcf,qfd->sqcd", hidden, w_down, preferred_element_type=jnp.float32)
    partial_value = partial_value.astype(jnp.bfloat16)
    returned = lax.all_to_all(partial_value, "dp", split_axis=0, concat_axis=0, tiled=True)
    flat_rows = returned.reshape(experts_all * capacity, returned.shape[3])
    picked = flat_rows[flat_slot].astype(jnp.float32)
    scaled = picked * weights[:, None]
    return lax.psum_scatter(
        jnp.sum(scaled.reshape(tok_rows, TOP, returned.shape[3]), axis=1).astype(jnp.bfloat16),
        "expert",
        scatter_dimension=1,
        tiled=True,
    )


def solution(mesh):
    in_specs = (
        P("dp", "expert"),
        P("dp", None),
        P("dp", None),
        P("dp", "expert", None),
        P("dp", "expert", None),
        P("dp", "expert", None),
    )
    out_specs = P("dp", "expert")
    plan = on_block if (mesh.shape["dp"], mesh.shape["expert"]) == (16, 2) else on_device
    return jax.shard_map(plan, mesh=mesh, in_specs=in_specs, out_specs=out_specs, check_vma=False)
```

```python
import functools

import jax
import jax.numpy as jnp
from jax import lax
from jax.experimental import pallas as pl
from jax.experimental.pallas import tpu as pltpu
from jax.sharding import PartitionSpec as P

TOP = 8
AXES = ("dp", "expert")
F32, BF16 = jnp.float32, jnp.bfloat16

BIT = {"Z": 8, "z": 4, "a": 2, "b": 1}
HOP = {8: "Z", 4: "z", 12: "z", 2: "a", 10: "a", 6: "a", 14: "a", 1: "b", 9: "b", 5: "b", 13: "b", 3: "b", 11: "b", 7: "z", 15: "z"}
SPREAD = (8, 4, 1, 2, 3, 5, 6, 9, 10, 12, 11, 7, 13, 14, 15)


def link_pairs(link):
    pairs = []
    for here in range(32):
        along_x, along_y = 4, 1
        first = (here >> 1) & 1 == 0
        step = {"Z": 16, "z": 8, "core": 2, "a": along_x if first else along_y, "b": along_y if first else along_x}[link]
        pairs.append((here, here ^ step))
    return pairs


def hop(value, link):
    return lax.ppermute(value, AXES, link_pairs(link))


def silu(v):
    return v / (1.0 + jnp.exp(-v))


def hidden_kernel(slots, ring, *refs):
    groups = (len(refs) - 14) // 5
    count = 8 * groups
    own, across, refs = refs[: 4 * groups], refs[4 * groups : 5 * groups], refs[5 * groups :]
    pieces = list(own) + [a.at[q] for a in across for q in range(4)]
    (pos, w_gate, w_up, out), scratch = refs[:4], refs[4:]
    held, gates, ups, routed, hidden, pick, piece_sem, gate_sem, up_sem, out_sem = scratch
    core, side = lax.axis_index("dp") % 2, lax.axis_index("expert")
    experts, hid, width = w_gate.shape
    rows, half = pieces[0].shape
    blocks = count // 2
    hid_block = gates.shape[1]
    per_expert = hid // hid_block
    hid_steps = experts * per_expert

    def piece_copy(i):
        return pltpu.make_async_copy(pieces[i], held.at[i], piece_sem.at[i])

    def weight_copies(i):
        at, slot = pl.ds((i % per_expert) * hid_block, hid_block), i % ring
        return (
            pltpu.make_async_copy(w_gate.at[i // per_expert, at], gates.at[slot], gate_sem.at[slot]),
            pltpu.make_async_copy(w_up.at[i // per_expert, at], ups.at[slot], up_sem.at[slot]),
        )

    for i in range(count):
        piece_copy(i).start()
    for i in range(ring):
        for copy in weight_copies(i):
            copy.start()

    slot = lax.broadcasted_iota(jnp.int32, (slots, rows), 0).astype(F32)
    for block in range(blocks):
        for e in range(experts):
            line = block * experts + e
            pick[block, pl.ds(e * slots, slots), :] = jnp.where(slot == pos[line : line + 1, :], 1.0, 0.0).astype(BF16)

    for number in range(count):
        piece_copy(number).wait()
        a, b = (number % 4) // 2, number % 2
        first = (core == 0) if number < blocks else (core == 1)
        x, y = jnp.where(first, a, b), jnp.where(first, b, a)
        block = x + 2 * (number // 4)
        column = (y ^ side) * half
        chosen = pick[block]
        row = pl.multiple_of(block * slots, 16)
        cut = half // 4
        for part in range(4):
            got = jnp.dot(chosen, held[number, :, part * cut : (part + 1) * cut], preferred_element_type=F32).astype(BF16)
            to = pl.ds(pl.multiple_of(column + part * cut, cut), cut)
            for e in range(experts):
                routed[e, pl.ds(row, slots), to] = got[e * slots : (e + 1) * slots]

    def hid_step(i, carry):
        for copy in weight_copies(i):
            copy.wait()
        e, slot = i // per_expert, i % ring
        at = pl.multiple_of((i % per_expert) * hid_block, hid_block)
        contract = (((1,), (1,)), ((), ()))
        gate = lax.dot_general(routed[e], gates[slot], contract, preferred_element_type=F32)
        up = lax.dot_general(routed[e], ups[slot], contract, preferred_element_type=F32)
        hidden[e, :, pl.ds(at, hid_block)] = (silu(gate) * up).astype(BF16)

        @pl.when(i + ring < hid_steps)
        def _():
            for copy in weight_copies(i + ring):
                copy.start()

        return carry

    lax.fori_loop(0, hid_steps, hid_step, 0)
    done = pltpu.make_async_copy(hidden, out, out_sem)
    done.start()
    done.wait()


def output_kernel(slots, groups, *refs):
    pos, weight, given, w_down, mine = refs[:5]
    others, scratch = refs[5 : 5 + groups], refs[5 + groups :]
    hidden, downs, put, scale, stage, given_sem, down_sem, out_sem = scratch
    side = lax.axis_index("expert")
    experts, hid, width = w_down.shape
    _, _, rows, half = mine.shape
    col_block = downs.shape[3]
    half_steps = half // col_block
    col_steps = width // col_block
    blocks = 4 * groups

    def down_copy(c):
        at = pl.ds(pl.multiple_of(c * col_block, col_block), col_block)
        return pltpu.make_async_copy(w_down.at[:, :, at], downs.at[c], down_sem.at[c])

    def out_copies(c):
        to, slot = (c // half_steps) ^ side, c % 2
        at = pl.ds(pl.multiple_of((c % half_steps) * col_block, col_block), col_block)
        copies = [pltpu.make_async_copy(stage.at[slot, pl.ds(0, 2 * groups)], mine.at[:, to, :, at], out_sem.at[slot, 0])]
        for g, other in enumerate(others):
            part = stage.at[slot, pl.ds(2 * groups + 2 * g, 2)]
            copies.append(pltpu.make_async_copy(part, other.at[:, to, :, at], out_sem.at[slot, 1 + g]))
        return copies

    given_copy = pltpu.make_async_copy(given, hidden, given_sem)
    given_copy.start()
    for c in range(col_steps):
        down_copy(c).start()

    slot = lax.broadcasted_iota(jnp.int32, (slots, rows), 0).astype(F32)
    for block in range(blocks):
        picks = []
        for e in range(experts):
            line = block * experts + e
            chosen = jnp.where(slot == pos[line : line + 1, :], 1.0, 0.0)
            scale[e, pl.ds(block * slots, slots), :] = jnp.sum(chosen * weight[line : line + 1, :], axis=1, keepdims=True)
            picks.append(chosen)
        put[block] = jnp.concatenate(picks, axis=0).T.astype(BF16)
    given_copy.wait()

    def col_step(c, carry):
        down_copy(c).wait()

        @pl.when(c >= 2)
        def _():
            for copy in out_copies(c - 2):
                copy.wait()

        outs = []
        for e in range(experts):
            part = jnp.dot(hidden[e], downs[c, e], preferred_element_type=F32)
            outs.append((part * scale[e]).astype(BF16))
        for block in range(blocks):
            these = jnp.concatenate([o[block * slots : (block + 1) * slots] for o in outs], axis=0)
            stage[c % 2, block] = jnp.dot(put[block], these, preferred_element_type=F32).astype(BF16)
        for copy in out_copies(c):
            copy.start()
        return carry

    lax.fori_loop(0, col_steps, col_step, 0)
    for c in (col_steps - 2, col_steps - 1):
        for copy in out_copies(c):
            copy.wait()


ANYWHERE = pl.BlockSpec(memory_space=pl.ANY)
IN_VMEM = pl.BlockSpec(memory_space=pltpu.VMEM)


def run_hidden(own, across, pos, w_gate, w_up, slots):
    experts, hid, width = w_gate.shape
    rows, half = own[0].shape
    hid_block, ring = 256, 3
    count = 2 * len(own)
    blocks = count // 2
    used = blocks * slots
    return pl.pallas_call(
        functools.partial(hidden_kernel, slots, ring),
        out_shape=jax.ShapeDtypeStruct((experts, used, hid), BF16),
        in_specs=[ANYWHERE] * (len(own) + len(across)) + [IN_VMEM] + [ANYWHERE] * 2,
        out_specs=ANYWHERE,
        scratch_shapes=[
            pltpu.VMEM((count, rows, half), BF16),
            pltpu.VMEM((ring, hid_block, width), BF16),
            pltpu.VMEM((ring, hid_block, width), BF16),
            pltpu.VMEM((experts, used, width), BF16),
            pltpu.VMEM((experts, used, hid), BF16),
            pltpu.VMEM((blocks, experts * slots, rows), BF16),
            pltpu.SemaphoreType.DMA((count,)),
            pltpu.SemaphoreType.DMA((ring,)),
            pltpu.SemaphoreType.DMA((ring,)),
            pltpu.SemaphoreType.DMA,
        ],
        compiler_params=pltpu.CompilerParams(vmem_limit_bytes=48 << 20),
        cost_estimate=pl.CostEstimate(
            flops=4 * experts * used * hid * width,
            bytes_accessed=4 * experts * hid * width + 2 * count * rows * half,
            transcendentals=experts * used * hid,
        ),
        name="hidden_units",
    )(*own, *across, pos, w_gate, w_up)


def run_outputs(hidden, pos, weight, w_down, slots, half):
    experts, hid, width = w_down.shape
    lines, rows = pos.shape
    col_block = 512
    blocks = lines // experts
    groups = blocks // 4
    used = blocks * slots
    mine = jax.ShapeDtypeStruct((2 * groups, 2, rows, half), BF16)
    other = jax.ShapeDtypeStruct((2, 2, rows, half), BF16)
    return pl.pallas_call(
        functools.partial(output_kernel, slots, groups),
        out_shape=(mine,) + (other,) * groups,
        in_specs=[IN_VMEM] * 2 + [ANYWHERE] * 2,
        out_specs=(ANYWHERE,) * (1 + groups),
        scratch_shapes=[
            pltpu.VMEM((experts, used, hid), BF16),
            pltpu.VMEM((width // col_block, experts, hid, col_block), BF16),
            pltpu.VMEM((blocks, rows, experts * slots), BF16),
            pltpu.VMEM((experts, used, 1), F32),
            pltpu.VMEM((2, blocks, rows, col_block), BF16),
            pltpu.SemaphoreType.DMA,
            pltpu.SemaphoreType.DMA((width // col_block,)),
            pltpu.SemaphoreType.DMA((2, 1 + groups)),
        ],
        compiler_params=pltpu.CompilerParams(vmem_limit_bytes=48 << 20),
        cost_estimate=pl.CostEstimate(
            flops=2 * experts * used * hid * width,
            bytes_accessed=2 * experts * hid * width + 4 * blocks * rows * half,
            transcendentals=0,
        ),
        name="weighted_outputs",
    )(pos, weight, hidden, w_down)


def slot_tables(expert_ids, gate_prob, experts_all):
    named = expert_ids[:, :, None] == jnp.arange(experts_all, dtype=jnp.int32)[None, None, :]
    chosen = jnp.any(named, axis=1)
    weight = jnp.sum(jnp.where(named, gate_prob[:, :, None], 0.0), axis=1)
    rows = expert_ids.shape[0]
    earlier = jnp.tril(jnp.ones((rows, rows), BF16), -1)
    before = jnp.dot(earlier, chosen.astype(BF16), preferred_element_type=F32)
    slot = jnp.where(chosen, before, -1.0)
    return jnp.stack([slot.T, weight.T], axis=1)


SPREAD_AFTER = (
    (4, ()),
    (8, ()),
    (2, ()),
    (1, ()),
    (3, ()),
    ('tables', (1, 2)),
    (5, (8,)),
    (6, (8,)),
    (10, (4,)),
    (12, ()),
    (7, (3, 8)),
    (11, (5,)),
    (('c', 0), ()),
    (9, (10, 5)),
    (('c', 4), ()),
    (13, (11, 6)),
    (14, (11, 6)),
    (15, (7,)),
)

COLLECT_AFTER = (
    (15, ()),
    (13, ()),
    (14, ()),
    (9, ()),
    (11, ()),
    (12, ()),
    (7, ()),
    (5, ()),
    (6, ()),
    (10, ()),
    (8, ()),
    (1, ()),
    (3, ()),
    (4, ()),
    (2, ()),
)


def after(value, *earlier):
    return lax.optimization_barrier((value, *earlier))[0] if earlier else value


def on_block(tokens, expert_ids, gate_prob, w_gate, w_up, w_down):
    dp_count, me = lax.axis_size("dp"), lax.axis_index("dp")
    rows, half = tokens.shape
    experts = w_gate.shape[0]
    experts_all = experts * dp_count
    capacity = 3 * rows * TOP // (2 * experts_all)
    slots = -(-capacity // 16) * 16
    core = me % 2

    held = {0: tokens}

    def tables_after(*earlier):
        own = after(slot_tables(expert_ids, gate_prob, experts_all), *earlier)
        every = lax.all_to_all(
            own.reshape(dp_count, experts, 2, rows), "dp", split_axis=0, concat_axis=0, tiled=True
        )
        return every[me ^ jnp.arange(dp_count, dtype=jnp.int32)]

    def tables_of(groups):
        order = [group | b for group in groups for b in (0, 2)]
        chosen = jnp.stack([held["tables"][r] for r in order + [r | 1 for r in order]])
        return chosen[:, :, 0].reshape(-1, rows), chosen[:, :, 1].reshape(-1, rows)

    def hidden_of(groups, *earlier):
        own = [held[group | q] for group in groups for q in range(4)]
        others = [held["c", group] for group in groups]
        return run_hidden(own, others, after(tables_of(groups)[0], *earlier), w_gate, w_up, slots)

    def outputs_of(groups, hidden, *earlier):
        pos, weight = tables_of(groups)
        mine, *others = run_outputs(hidden, after(pos, *earlier), weight, w_down, slots, half)
        return mine.reshape(-1, 4, rows, half), others

    sums, received = {}, {}

    def add_swapped(groups, mine, others, *earlier):
        for n, group in enumerate(groups):
            back = received["c", group] = hop(after(others[n], *earlier), "core")
            back = back.reshape(4, rows, half)
            for q in range(4):
                at = jnp.where(core == 0, q, (q % 2) * 2 + q // 2)
                sums[group | q] = [lax.dynamic_index_in_dim(v, at, 0, keepdims=False) for v in (mine[n], back)]

    def total(j):
        terms = sums[j] + [received[k] for k in SPREAD if k & ~BIT[HOP[k]] == j]
        return sum(t.astype(F32) for t in terms).astype(BF16)

    def spread_all(plan, *fence):
        for j, earlier in plan:
            earlier = [held[k] for k in earlier] + list(fence)
            if j == "tables":
                held[j] = tables_after(*earlier)
            elif isinstance(j, tuple):
                pieces = [after(held[j[1] | q], *earlier) if q else held[j[1]] for q in range(4)]
                held[j] = hop(jnp.stack(pieces), "core")
            else:
                held[j] = hop(after(held[j & ~BIT[HOP[j]]], *earlier), HOP[j])

    def collect_all(plan, *fence):
        for j, earlier in plan:
            earlier = [received[k] for k in earlier] + list(fence)
            received[j] = hop(after(total(j), *earlier), HOP[j])

    spread_all(SPREAD_AFTER)
    near = hidden_of((0, 4))
    spread_all([(("c", 8), ()), (("c", 12), ())], near)
    far = hidden_of((12, 8))
    mine, others = outputs_of((12, 8), far)
    add_swapped((12, 8), mine, others)
    mine, others = outputs_of((0, 4), near, received["c", 12])
    add_swapped((0, 4), mine, others)
    collect_all(COLLECT_AFTER)
    return total(0)


def on_device(tokens, expert_ids, gate_prob, w_gate, w_up, w_down):
    dp_count = lax.axis_size("dp")
    tok_rows = tokens.shape[0]
    local_experts = w_gate.shape[0]
    experts_all = local_experts * dp_count
    capacity = 3 * tok_rows * TOP // (2 * experts_all)
    flat_ids = expert_ids.reshape(-1)
    pair_count = flat_ids.shape[0]
    onehot = (flat_ids[:, None] == jnp.arange(experts_all, dtype=jnp.int32)[None, :]).astype(
        jnp.int32
    )
    before = jnp.cumsum(onehot, axis=0, dtype=jnp.int32) - onehot
    slot_pos = jnp.sum(before * onehot, axis=1, dtype=jnp.int32)
    flat_slot = flat_ids * capacity + slot_pos
    owner_row = jnp.arange(pair_count, dtype=jnp.int32) // TOP
    source_row = (
        jnp.full((experts_all * capacity,), tok_rows, jnp.int32).at[flat_slot].set(owner_row)
    )
    weights = gate_prob.reshape(-1)
    gathered = lax.all_gather(tokens, "expert", axis=1, tiled=True)
    padded = jnp.concatenate([gathered, jnp.zeros((1, gathered.shape[1]), gathered.dtype)], axis=0)
    arrived = lax.all_to_all(
        padded[source_row].reshape(dp_count, local_experts, capacity, gathered.shape[1]),
        "dp",
        split_axis=0,
        concat_axis=0,
        tiled=True,
    )
    gate_sum = jnp.einsum("sqcd,qfd->sqcf", arrived, w_gate, preferred_element_type=jnp.float32)
    up_sum = jnp.einsum("sqcd,qfd->sqcf", arrived, w_up, preferred_element_type=jnp.float32)
    hidden = (jax.nn.silu(gate_sum) * up_sum).astype(jnp.bfloat16)
    partial_value = jnp.einsum("sqcf,qfd->sqcd", hidden, w_down, preferred_element_type=jnp.float32)
    partial_value = partial_value.astype(jnp.bfloat16)
    returned = lax.all_to_all(partial_value, "dp", split_axis=0, concat_axis=0, tiled=True)
    flat_rows = returned.reshape(experts_all * capacity, returned.shape[3])
    picked = flat_rows[flat_slot].astype(jnp.float32)
    scaled = picked * weights[:, None]
    return lax.psum_scatter(
        jnp.sum(scaled.reshape(tok_rows, TOP, returned.shape[3]), axis=1).astype(jnp.bfloat16),
        "expert",
        scatter_dimension=1,
        tiled=True,
    )


def solution(mesh):
    in_specs = (
        P("dp", "expert"),
        P("dp", None),
        P("dp", None),
        P("dp", "expert", None),
        P("dp", "expert", None),
        P("dp", "expert", None),
    )
    out_specs = P("dp", "expert")
    plan = on_block if (mesh.shape["dp"], mesh.shape["expert"]) == (16, 2) else on_device
    return jax.shard_map(plan, mesh=mesh, in_specs=in_specs, out_specs=out_specs, check_vma=False)
```

```python
import functools

import jax
import jax.numpy as jnp
from jax import lax
from jax.experimental import pallas as pl
from jax.experimental.pallas import tpu as pltpu
from jax.sharding import PartitionSpec as P

TOP = 8
AXES = ("dp", "expert")
F32, BF16 = jnp.float32, jnp.bfloat16

BIT = {"Z": 8, "z": 4, "a": 2, "b": 1}
HOP = {8: "Z", 4: "z", 12: "z", 2: "a", 10: "a", 6: "a", 14: "a", 1: "b", 9: "b", 5: "b", 13: "b", 3: "b", 11: "b", 7: "z", 15: "z"}
SPREAD = (8, 4, 1, 2, 3, 5, 6, 9, 10, 12, 11, 7, 13, 14, 15)


def link_pairs(link):
    pairs = []
    for here in range(32):
        along_x, along_y = 4, 1
        first = (here >> 1) & 1 == 0
        step = {"Z": 16, "z": 8, "core": 2, "a": along_x if first else along_y, "b": along_y if first else along_x}[link]
        pairs.append((here, here ^ step))
    return pairs


def hop(value, link):
    return lax.ppermute(value, AXES, link_pairs(link))


def silu(v):
    return v / (1.0 + jnp.exp(-v))


def hidden_kernel(slots, ring, *refs):
    groups = (len(refs) - 13) // 5
    count = 8 * groups
    own, across, refs = refs[: 4 * groups], refs[4 * groups : 5 * groups], refs[5 * groups :]
    pieces = list(own) + [a.at[q] for a in across for q in range(4)]
    (pos, w_gate, w_up, out), scratch = refs[:4], refs[4:]
    held, both, routed, hidden, pick, piece_sem, gate_sem, up_sem, out_sem = scratch
    core, side = lax.axis_index("dp") % 2, lax.axis_index("expert")
    experts, hid, width = w_gate.shape
    rows, half = pieces[0].shape
    blocks = count // 2
    hid_block = both.shape[1] // 2
    per_expert = hid // hid_block
    hid_steps = experts * per_expert

    def piece_copy(i):
        return pltpu.make_async_copy(pieces[i], held.at[i], piece_sem.at[i])

    def weight_copies(i):
        at, slot = pl.ds((i % per_expert) * hid_block, hid_block), i % ring
        return (
            pltpu.make_async_copy(w_gate.at[i // per_expert, at], both.at[slot, pl.ds(0, hid_block)], gate_sem.at[slot]),
            pltpu.make_async_copy(w_up.at[i // per_expert, at], both.at[slot, pl.ds(hid_block, hid_block)], up_sem.at[slot]),
        )

    for i in range(count):
        piece_copy(i).start()
    for i in range(ring):
        for copy in weight_copies(i):
            copy.start()

    slot = lax.broadcasted_iota(jnp.int32, (slots, rows), 0).astype(F32)
    for block in range(blocks):
        for e in range(experts):
            line = block * experts + e
            pick[block, pl.ds(e * slots, slots), :] = jnp.where(slot == pos[line : line + 1, :], 1.0, 0.0).astype(BF16)

    for number in range(count):
        piece_copy(number).wait()
        a, b = (number % 4) // 2, number % 2
        first = (core == 0) if number < blocks else (core == 1)
        x, y = jnp.where(first, a, b), jnp.where(first, b, a)
        block = x + 2 * (number // 4)
        column = (y ^ side) * half
        chosen = pick[block]
        row = pl.multiple_of(block * slots, 16)
        cut = half // 4
        for part in range(4):
            got = jnp.dot(chosen, held[number, :, part * cut : (part + 1) * cut], preferred_element_type=F32).astype(BF16)
            to = pl.ds(pl.multiple_of(column + part * cut, cut), cut)
            for e in range(experts):
                routed[e, pl.ds(row, slots), to] = got[e * slots : (e + 1) * slots]

    def hid_step(i, carry):
        for copy in weight_copies(i):
            copy.wait()
        e, slot = i // per_expert, i % ring
        at = pl.multiple_of((i % per_expert) * hid_block, hid_block)
        contract = (((1,), (1,)), ((), ()))
        gate_up = lax.dot_general(routed[e], both[slot], contract, preferred_element_type=F32)
        gate, up = gate_up[:, :hid_block], gate_up[:, hid_block:]
        hidden[e, :, pl.ds(at, hid_block)] = (silu(gate) * up).astype(BF16)

        @pl.when(i + ring < hid_steps)
        def _():
            for copy in weight_copies(i + ring):
                copy.start()

        return carry

    lax.fori_loop(0, hid_steps, hid_step, 0)
    done = pltpu.make_async_copy(hidden, out, out_sem)
    done.start()
    done.wait()


def output_kernel(slots, groups, *refs):
    pos, weight, given, w_down, mine = refs[:5]
    others, scratch = refs[5 : 5 + groups], refs[5 + groups :]
    hidden, downs, put, scale, stage, given_sem, down_sem, out_sem = scratch
    side = lax.axis_index("expert")
    experts, hid, width = w_down.shape
    _, _, rows, half = mine.shape
    col_block = downs.shape[3]
    half_steps = half // col_block
    col_steps = width // col_block
    blocks = 4 * groups

    def down_copy(c):
        at = pl.ds(pl.multiple_of(c * col_block, col_block), col_block)
        return pltpu.make_async_copy(w_down.at[:, :, at], downs.at[c], down_sem.at[c])

    def out_copies(c):
        to, slot = (c // half_steps) ^ side, c % 2
        at = pl.ds(pl.multiple_of((c % half_steps) * col_block, col_block), col_block)
        copies = [pltpu.make_async_copy(stage.at[slot, pl.ds(0, 2 * groups)], mine.at[:, to, :, at], out_sem.at[slot, 0])]
        for g, other in enumerate(others):
            part = stage.at[slot, pl.ds(2 * groups + 2 * g, 2)]
            copies.append(pltpu.make_async_copy(part, other.at[:, to, :, at], out_sem.at[slot, 1 + g]))
        return copies

    given_copy = pltpu.make_async_copy(given, hidden, given_sem)
    given_copy.start()
    for c in range(col_steps):
        down_copy(c).start()

    slot = lax.broadcasted_iota(jnp.int32, (slots, rows), 0).astype(F32)
    for block in range(blocks):
        picks = []
        for e in range(experts):
            line = block * experts + e
            chosen = jnp.where(slot == pos[line : line + 1, :], 1.0, 0.0)
            scale[e, pl.ds(block * slots, slots), :] = jnp.sum(chosen * weight[line : line + 1, :], axis=1, keepdims=True)
            picks.append(chosen)
        put[block] = jnp.concatenate(picks, axis=0).T.astype(BF16)
    given_copy.wait()

    def col_step(c, carry):
        down_copy(c).wait()

        @pl.when(c >= 2)
        def _():
            for copy in out_copies(c - 2):
                copy.wait()

        outs = []
        for e in range(experts):
            part = jnp.dot(hidden[e], downs[c, e], preferred_element_type=F32)
            outs.append((part * scale[e]).astype(BF16))
        for block in range(blocks):
            these = jnp.concatenate([o[block * slots : (block + 1) * slots] for o in outs], axis=0)
            stage[c % 2, block] = jnp.dot(put[block], these, preferred_element_type=F32).astype(BF16)
        for copy in out_copies(c):
            copy.start()
        return carry

    lax.fori_loop(0, col_steps, col_step, 0)
    for c in (col_steps - 2, col_steps - 1):
        for copy in out_copies(c):
            copy.wait()


ANYWHERE = pl.BlockSpec(memory_space=pl.ANY)
IN_VMEM = pl.BlockSpec(memory_space=pltpu.VMEM)


def run_hidden(own, across, pos, w_gate, w_up, slots):
    experts, hid, width = w_gate.shape
    rows, half = own[0].shape
    hid_block, ring = 256, 3
    count = 2 * len(own)
    blocks = count // 2
    used = blocks * slots
    return pl.pallas_call(
        functools.partial(hidden_kernel, slots, ring),
        out_shape=jax.ShapeDtypeStruct((experts, used, hid), BF16),
        in_specs=[ANYWHERE] * (len(own) + len(across)) + [IN_VMEM] + [ANYWHERE] * 2,
        out_specs=ANYWHERE,
        scratch_shapes=[
            pltpu.VMEM((count, rows, half), BF16),
            pltpu.VMEM((ring, 2 * hid_block, width), BF16),
            pltpu.VMEM((experts, used, width), BF16),
            pltpu.VMEM((experts, used, hid), BF16),
            pltpu.VMEM((blocks, experts * slots, rows), BF16),
            pltpu.SemaphoreType.DMA((count,)),
            pltpu.SemaphoreType.DMA((ring,)),
            pltpu.SemaphoreType.DMA((ring,)),
            pltpu.SemaphoreType.DMA,
        ],
        compiler_params=pltpu.CompilerParams(vmem_limit_bytes=40 << 20),
        cost_estimate=pl.CostEstimate(
            flops=4 * experts * used * hid * width,
            bytes_accessed=4 * experts * hid * width + 2 * count * rows * half,
            transcendentals=experts * used * hid,
        ),
        name="hidden_units",
    )(*own, *across, pos, w_gate, w_up)


def run_outputs(hidden, pos, weight, w_down, slots, half):
    experts, hid, width = w_down.shape
    lines, rows = pos.shape
    col_block = 512
    blocks = lines // experts
    groups = blocks // 4
    used = blocks * slots
    mine = jax.ShapeDtypeStruct((2 * groups, 2, rows, half), BF16)
    other = jax.ShapeDtypeStruct((2, 2, rows, half), BF16)
    return pl.pallas_call(
        functools.partial(output_kernel, slots, groups),
        out_shape=(mine,) + (other,) * groups,
        in_specs=[IN_VMEM] * 2 + [ANYWHERE] * 2,
        out_specs=(ANYWHERE,) * (1 + groups),
        scratch_shapes=[
            pltpu.VMEM((experts, used, hid), BF16),
            pltpu.VMEM((width // col_block, experts, hid, col_block), BF16),
            pltpu.VMEM((blocks, rows, experts * slots), BF16),
            pltpu.VMEM((experts, used, 1), F32),
            pltpu.VMEM((2, blocks, rows, col_block), BF16),
            pltpu.SemaphoreType.DMA,
            pltpu.SemaphoreType.DMA((width // col_block,)),
            pltpu.SemaphoreType.DMA((2, 1 + groups)),
        ],
        compiler_params=pltpu.CompilerParams(vmem_limit_bytes=40 << 20),
        cost_estimate=pl.CostEstimate(
            flops=16 * experts * used * hid * width,
            bytes_accessed=2 * experts * hid * width + 4 * blocks * rows * half,
            transcendentals=0,
        ),
        name="weighted_outputs",
    )(pos, weight, hidden, w_down)


def slot_tables(expert_ids, gate_prob, experts_all):
    named = expert_ids[:, :, None] == jnp.arange(experts_all, dtype=jnp.int32)[None, None, :]
    chosen = jnp.any(named, axis=1)
    weight = jnp.sum(jnp.where(named, gate_prob[:, :, None], 0.0), axis=1)
    rows = expert_ids.shape[0]
    earlier = jnp.tril(jnp.ones((rows, rows), BF16), -1)
    before = jnp.dot(earlier, chosen.astype(BF16), preferred_element_type=F32)
    slot = jnp.where(chosen, before, -1.0)
    return jnp.stack([slot.T, weight.T], axis=1)


SPREAD_AFTER = (
    (4, ()),
    (8, ()),
    (2, ()),
    (1, ()),
    (3, ()),
    ('tables', (1, 2)),
    (5, (8, 'tables')),
    (6, (8,)),
    (10, (4,)),
    (12, ()),
    (7, (3, 8)),
    (11, ()),
    (('c', 0), ()),
    (9, (10, 5)),
    (('c', 4), ()),
    (13, (11, 6)),
    (14, (11, 6)),
    (15, (7,)),
)

COLLECT_AFTER = (
    (15, ()),
    (13, ()),
    (14, ()),
    (9, ()),
    (11, ()),
    (12, (('c', 8),)),
    (7, ()),
    (5, ()),
    (6, (('c', 4), ('c', 8))),
    (10, ()),
    (8, ()),
    (1, ()),
    (3, ()),
    (4, ()),
    (2, ()),
)


def after(value, *earlier):
    return lax.optimization_barrier((value, *earlier))[0] if earlier else value


def on_block(tokens, expert_ids, gate_prob, w_gate, w_up, w_down):
    dp_count, me = lax.axis_size("dp"), lax.axis_index("dp")
    rows, half = tokens.shape
    experts = w_gate.shape[0]
    experts_all = experts * dp_count
    capacity = 3 * rows * TOP // (2 * experts_all)
    slots = -(-capacity // 16) * 16
    core = me % 2

    held = {0: tokens}

    def tables_after(*earlier):
        own = after(slot_tables(expert_ids, gate_prob, experts_all), *earlier)
        every = lax.all_to_all(
            own.reshape(dp_count, experts, 2, rows), "dp", split_axis=0, concat_axis=0, tiled=True
        )
        return every[me ^ jnp.arange(dp_count, dtype=jnp.int32)]

    def tables_of(groups):
        order = [group | b for group in groups for b in (0, 2)]
        chosen = jnp.stack([held["tables"][r] for r in order + [r | 1 for r in order]])
        return chosen[:, :, 0].reshape(-1, rows), chosen[:, :, 1].reshape(-1, rows)

    def hidden_of(groups, *earlier):
        own = [held[group | q] for group in groups for q in range(4)]
        others = [held["c", group] for group in groups]
        return run_hidden(own, others, after(tables_of(groups)[0], *earlier), w_gate, w_up, slots)

    def outputs_of(groups, hidden, *earlier):
        pos, weight = tables_of(groups)
        mine, *others = run_outputs(hidden, after(pos, *earlier), weight, w_down, slots, half)
        return mine.reshape(-1, 4, rows, half), others

    sums, received = {}, {}

    def add_swapped(groups, mine, others, *earlier):
        for n, group in enumerate(groups):
            back = received["c", group] = hop(after(others[n], *earlier), "core")
            back = back.reshape(4, rows, half)
            for q in range(4):
                at = jnp.where(core == 0, q, (q % 2) * 2 + q // 2)
                sums[group | q] = [lax.dynamic_index_in_dim(v, at, 0, keepdims=False) for v in (mine[n], back)]

    def total(j):
        terms = sums[j] + [received[k] for k in SPREAD if k & ~BIT[HOP[k]] == j]
        return sum(t.astype(F32) for t in terms).astype(BF16)

    def spread_all(plan, *fence):
        for j, earlier in plan:
            earlier = [held[k] for k in earlier] + list(fence)
            if j == "tables":
                held[j] = tables_after(*earlier)
            elif isinstance(j, tuple):
                pieces = [after(held[j[1] | q], *earlier) if q else held[j[1]] for q in range(4)]
                held[j] = hop(jnp.stack(pieces), "core")
            else:
                held[j] = hop(after(held[j & ~BIT[HOP[j]]], *earlier), HOP[j])

    def collect_all(plan, *fence):
        for j, earlier in plan:
            earlier = [received[k] for k in earlier] + list(fence)
            received[j] = hop(after(total(j), *earlier), HOP[j])

    spread_all(SPREAD_AFTER)
    near = hidden_of((0, 4))
    spread_all([(("c", 8), ()), (("c", 12), ())], near)
    far = hidden_of((12, 8))
    mine, others = outputs_of((12, 8), far)
    add_swapped((12, 8), mine, others)
    mine, others = outputs_of((0, 4), near, received["c", 12])
    add_swapped((0, 4), mine, others)
    collect_all(COLLECT_AFTER)
    return total(0)


def on_device(tokens, expert_ids, gate_prob, w_gate, w_up, w_down):
    dp_count = lax.axis_size("dp")
    tok_rows = tokens.shape[0]
    local_experts = w_gate.shape[0]
    experts_all = local_experts * dp_count
    capacity = 3 * tok_rows * TOP // (2 * experts_all)
    flat_ids = expert_ids.reshape(-1)
    pair_count = flat_ids.shape[0]
    onehot = (flat_ids[:, None] == jnp.arange(experts_all, dtype=jnp.int32)[None, :]).astype(
        jnp.int32
    )
    before = jnp.cumsum(onehot, axis=0, dtype=jnp.int32) - onehot
    slot_pos = jnp.sum(before * onehot, axis=1, dtype=jnp.int32)
    flat_slot = flat_ids * capacity + slot_pos
    owner_row = jnp.arange(pair_count, dtype=jnp.int32) // TOP
    source_row = (
        jnp.full((experts_all * capacity,), tok_rows, jnp.int32).at[flat_slot].set(owner_row)
    )
    weights = gate_prob.reshape(-1)
    gathered = lax.all_gather(tokens, "expert", axis=1, tiled=True)
    padded = jnp.concatenate([gathered, jnp.zeros((1, gathered.shape[1]), gathered.dtype)], axis=0)
    arrived = lax.all_to_all(
        padded[source_row].reshape(dp_count, local_experts, capacity, gathered.shape[1]),
        "dp",
        split_axis=0,
        concat_axis=0,
        tiled=True,
    )
    gate_sum = jnp.einsum("sqcd,qfd->sqcf", arrived, w_gate, preferred_element_type=jnp.float32)
    up_sum = jnp.einsum("sqcd,qfd->sqcf", arrived, w_up, preferred_element_type=jnp.float32)
    hidden = (jax.nn.silu(gate_sum) * up_sum).astype(jnp.bfloat16)
    partial_value = jnp.einsum("sqcf,qfd->sqcd", hidden, w_down, preferred_element_type=jnp.float32)
    partial_value = partial_value.astype(jnp.bfloat16)
    returned = lax.all_to_all(partial_value, "dp", split_axis=0, concat_axis=0, tiled=True)
    flat_rows = returned.reshape(experts_all * capacity, returned.shape[3])
    picked = flat_rows[flat_slot].astype(jnp.float32)
    scaled = picked * weights[:, None]
    return lax.psum_scatter(
        jnp.sum(scaled.reshape(tok_rows, TOP, returned.shape[3]), axis=1).astype(jnp.bfloat16),
        "expert",
        scatter_dimension=1,
        tiled=True,
    )


def solution(mesh):
    in_specs = (
        P("dp", "expert"),
        P("dp", None),
        P("dp", None),
        P("dp", "expert", None),
        P("dp", "expert", None),
        P("dp", "expert", None),
    )
    out_specs = P("dp", "expert")
    plan = on_block if (mesh.shape["dp"], mesh.shape["expert"]) == (16, 2) else on_device
    return jax.shard_map(plan, mesh=mesh, in_specs=in_specs, out_specs=out_specs, check_vma=False)
```

```python
import functools

import jax
import jax.numpy as jnp
from jax import lax
from jax.experimental import pallas as pl
from jax.experimental.pallas import tpu as pltpu
from jax.sharding import PartitionSpec as P

TOP = 8
AXES = ("dp", "expert")
F32, BF16 = jnp.float32, jnp.bfloat16

BIT = {"Z": 8, "z": 4, "a": 2, "b": 1}
HOP = {8: "Z", 4: "z", 12: "z", 2: "a", 10: "a", 6: "a", 14: "a", 1: "b", 9: "b", 5: "b", 13: "b", 3: "b", 11: "b", 7: "z", 15: "z"}
SPREAD = (8, 4, 1, 2, 3, 5, 6, 9, 10, 12, 11, 7, 13, 14, 15)


def link_pairs(link):
    pairs = []
    for here in range(32):
        along_x, along_y = 4, 1
        first = (here >> 1) & 1 == 0
        step = {"Z": 16, "z": 8, "core": 2, "a": along_x if first else along_y, "b": along_y if first else along_x}[link]
        pairs.append((here, here ^ step))
    return pairs


def hop(value, link):
    return lax.ppermute(value, AXES, link_pairs(link))


def silu(v):
    return v / (1.0 + jnp.exp(-v))


def hidden_kernel(slots, ring, *refs):
    groups = (len(refs) - 13) // 5
    count = 8 * groups
    own, across, refs = refs[: 4 * groups], refs[4 * groups : 5 * groups], refs[5 * groups :]
    pieces = list(own) + [a.at[q] for a in across for q in range(4)]
    (pos, w_gate, w_up, out), scratch = refs[:4], refs[4:]
    held, both, routed, hidden, pick, piece_sem, gate_sem, up_sem, out_sem = scratch
    core, side = lax.axis_index("dp") % 2, lax.axis_index("expert")
    experts, hid, width = w_gate.shape
    rows, half = pieces[0].shape
    blocks = count // 2
    hid_block = both.shape[1] // 2
    per_expert = hid // hid_block
    hid_steps = experts * per_expert

    def piece_copy(i):
        return pltpu.make_async_copy(pieces[i], held.at[i], piece_sem.at[i])

    def weight_copies(i):
        at, slot = pl.ds((i % per_expert) * hid_block, hid_block), i % ring
        return (
            pltpu.make_async_copy(w_gate.at[i // per_expert, at], both.at[slot, pl.ds(0, hid_block)], gate_sem.at[slot]),
            pltpu.make_async_copy(w_up.at[i // per_expert, at], both.at[slot, pl.ds(hid_block, hid_block)], up_sem.at[slot]),
        )

    for i in range(count):
        piece_copy(i).start()
    for i in range(ring):
        for copy in weight_copies(i):
            copy.start()

    slot = lax.broadcasted_iota(jnp.int32, (slots, rows), 0).astype(F32)
    for block in range(blocks):
        for e in range(experts):
            line = block * experts + e
            pick[block, pl.ds(e * slots, slots), :] = jnp.where(slot == pos[line : line + 1, :], 1.0, 0.0).astype(BF16)

    for number in range(count):
        piece_copy(number).wait()
        a, b = (number % 4) // 2, number % 2
        first = (core == 0) if number < blocks else (core == 1)
        x, y = jnp.where(first, a, b), jnp.where(first, b, a)
        block = x + 2 * (number // 4)
        column = (y ^ side) * half
        chosen = pick[block]
        row = pl.multiple_of(block * slots, 16)
        cut = half // 4
        for part in range(4):
            got = jnp.dot(chosen, held[number, :, part * cut : (part + 1) * cut], preferred_element_type=F32).astype(BF16)
            to = pl.ds(pl.multiple_of(column + part * cut, cut), cut)
            for e in range(experts):
                routed[e, pl.ds(row, slots), to] = got[e * slots : (e + 1) * slots]

    def hid_step(i, carry):
        for copy in weight_copies(i):
            copy.wait()
        e, slot = i // per_expert, i % ring
        at = pl.multiple_of((i % per_expert) * hid_block, hid_block)
        contract = (((1,), (1,)), ((), ()))
        gate_up = lax.dot_general(routed[e], both[slot], contract, preferred_element_type=F32)
        gate, up = gate_up[:, :hid_block], gate_up[:, hid_block:]
        hidden[e, :, pl.ds(at, hid_block)] = (silu(gate) * up).astype(BF16)

        @pl.when(i + ring < hid_steps)
        def _():
            for copy in weight_copies(i + ring):
                copy.start()

        return carry

    lax.fori_loop(0, hid_steps, hid_step, 0)
    done = pltpu.make_async_copy(hidden, out, out_sem)
    done.start()
    done.wait()


def output_kernel(slots, groups, *refs):
    pos, weight, given, w_down, mine = refs[:5]
    others, scratch = refs[5 : 5 + groups], refs[5 + groups :]
    hidden, downs, put, scale, stage, given_sem, down_sem, out_sem = scratch
    side = lax.axis_index("expert")
    experts, hid, width = w_down.shape
    _, _, rows, half = mine.shape
    col_block = downs.shape[3]
    half_steps = half // col_block
    col_steps = width // col_block
    blocks = 4 * groups

    def down_copy(c):
        at = pl.ds(pl.multiple_of(c * col_block, col_block), col_block)
        return pltpu.make_async_copy(w_down.at[:, :, at], downs.at[c], down_sem.at[c])

    def out_copies(c):
        to, slot = (c // half_steps) ^ side, c % 2
        at = pl.ds(pl.multiple_of((c % half_steps) * col_block, col_block), col_block)
        copies = [pltpu.make_async_copy(stage.at[slot, pl.ds(0, 2 * groups)], mine.at[:, to, :, at], out_sem.at[slot, 0])]
        for g, other in enumerate(others):
            part = stage.at[slot, pl.ds(2 * groups + 2 * g, 2)]
            copies.append(pltpu.make_async_copy(part, other.at[:, to, :, at], out_sem.at[slot, 1 + g]))
        return copies

    given_copy = pltpu.make_async_copy(given, hidden, given_sem)
    given_copy.start()
    for c in range(col_steps):
        down_copy(c).start()

    slot = lax.broadcasted_iota(jnp.int32, (slots, rows), 0).astype(F32)
    for block in range(blocks):
        picks = []
        for e in range(experts):
            line = block * experts + e
            chosen = jnp.where(slot == pos[line : line + 1, :], 1.0, 0.0)
            scale[e, pl.ds(block * slots, slots), :] = jnp.sum(chosen * weight[line : line + 1, :], axis=1, keepdims=True)
            picks.append(chosen)
        put[block] = jnp.concatenate(picks, axis=0).T.astype(BF16)
    given_copy.wait()

    def col_step(c, carry):
        down_copy(c).wait()

        @pl.when(c >= 2)
        def _():
            for copy in out_copies(c - 2):
                copy.wait()

        outs = []
        for e in range(experts):
            part = jnp.dot(hidden[e], downs[c, e], preferred_element_type=F32)
            outs.append((part * scale[e]).astype(BF16))
        for block in range(blocks):
            these = jnp.concatenate([o[block * slots : (block + 1) * slots] for o in outs], axis=0)
            stage[c % 2, block] = jnp.dot(put[block], these, preferred_element_type=F32).astype(BF16)
        for copy in out_copies(c):
            copy.start()
        return carry

    lax.fori_loop(0, col_steps, col_step, 0)
    for c in (col_steps - 2, col_steps - 1):
        for copy in out_copies(c):
            copy.wait()


ANYWHERE = pl.BlockSpec(memory_space=pl.ANY)
IN_VMEM = pl.BlockSpec(memory_space=pltpu.VMEM)


def run_hidden(own, across, pos, w_gate, w_up, slots):
    experts, hid, width = w_gate.shape
    rows, half = own[0].shape
    hid_block, ring = 256, 3
    count = 2 * len(own)
    blocks = count // 2
    used = blocks * slots
    return pl.pallas_call(
        functools.partial(hidden_kernel, slots, ring),
        out_shape=jax.ShapeDtypeStruct((experts, used, hid), BF16),
        in_specs=[ANYWHERE] * (len(own) + len(across)) + [IN_VMEM] + [ANYWHERE] * 2,
        out_specs=ANYWHERE,
        scratch_shapes=[
            pltpu.VMEM((count, rows, half), BF16),
            pltpu.VMEM((ring, 2 * hid_block, width), BF16),
            pltpu.VMEM((experts, used, width), BF16),
            pltpu.VMEM((experts, used, hid), BF16),
            pltpu.VMEM((blocks, experts * slots, rows), BF16),
            pltpu.SemaphoreType.DMA((count,)),
            pltpu.SemaphoreType.DMA((ring,)),
            pltpu.SemaphoreType.DMA((ring,)),
            pltpu.SemaphoreType.DMA,
        ],
        compiler_params=pltpu.CompilerParams(vmem_limit_bytes=40 << 20),
        cost_estimate=pl.CostEstimate(
            flops=4 * experts * used * hid * width,
            bytes_accessed=4 * experts * hid * width + 2 * count * rows * half,
            transcendentals=experts * used * hid,
        ),
        name="hidden_units",
    )(*own, *across, pos, w_gate, w_up)


def run_outputs(hidden, pos, weight, w_down, slots, half):
    experts, hid, width = w_down.shape
    lines, rows = pos.shape
    col_block = 1024
    blocks = lines // experts
    groups = blocks // 4
    used = blocks * slots
    mine = jax.ShapeDtypeStruct((2 * groups, 2, rows, half), BF16)
    other = jax.ShapeDtypeStruct((2, 2, rows, half), BF16)
    return pl.pallas_call(
        functools.partial(output_kernel, slots, groups),
        out_shape=(mine,) + (other,) * groups,
        in_specs=[IN_VMEM] * 2 + [ANYWHERE] * 2,
        out_specs=(ANYWHERE,) * (1 + groups),
        scratch_shapes=[
            pltpu.VMEM((experts, used, hid), BF16),
            pltpu.VMEM((width // col_block, experts, hid, col_block), BF16),
            pltpu.VMEM((blocks, rows, experts * slots), BF16),
            pltpu.VMEM((experts, used, 1), F32),
            pltpu.VMEM((2, blocks, rows, col_block), BF16),
            pltpu.SemaphoreType.DMA,
            pltpu.SemaphoreType.DMA((width // col_block,)),
            pltpu.SemaphoreType.DMA((2, 1 + groups)),
        ],
        compiler_params=pltpu.CompilerParams(vmem_limit_bytes=40 << 20),
        cost_estimate=pl.CostEstimate(
            flops=16 * experts * used * hid * width,
            bytes_accessed=2 * experts * hid * width + 4 * blocks * rows * half,
            transcendentals=0,
        ),
        name="weighted_outputs",
    )(pos, weight, hidden, w_down)


def slot_tables(expert_ids, gate_prob, experts_all):
    named = expert_ids[:, :, None] == jnp.arange(experts_all, dtype=jnp.int32)[None, None, :]
    chosen = jnp.any(named, axis=1)
    weight = jnp.sum(jnp.where(named, gate_prob[:, :, None], 0.0), axis=1)
    rows = expert_ids.shape[0]
    earlier = jnp.tril(jnp.ones((rows, rows), BF16), -1)
    before = jnp.dot(earlier, chosen.astype(BF16), preferred_element_type=F32)
    slot = jnp.where(chosen, before, -1.0)
    return jnp.stack([slot.T, weight.T], axis=1)


SPREAD_AFTER = (
    (4, ()),
    (8, ()),
    (2, ()),
    (1, ()),
    (3, ()),
    ('tables', (1, 2)),
    (5, (8, 'tables')),
    (6, (8,)),
    (10, (4,)),
    (12, ()),
    (7, (3, 8)),
    (11, ()),
    (('c', 0), ()),
    (9, (10, 5)),
    (('c', 4), ()),
    (13, (11, 6)),
    (14, (11, 6)),
    (15, (7,)),
)

COLLECT_AFTER = (
    (15, ()),
    (13, ()),
    (14, ()),
    (9, ()),
    (11, ()),
    (12, (('c', 8),)),
    (7, ()),
    (5, ()),
    (6, (('c', 4), ('c', 8))),
    (10, ()),
    (8, ()),
    (1, ()),
    (3, ()),
    (4, ()),
    (2, ()),
)


def after(value, *earlier):
    return lax.optimization_barrier((value, *earlier))[0] if earlier else value


def on_block(tokens, expert_ids, gate_prob, w_gate, w_up, w_down):
    dp_count, me = lax.axis_size("dp"), lax.axis_index("dp")
    rows, half = tokens.shape
    experts = w_gate.shape[0]
    experts_all = experts * dp_count
    capacity = 3 * rows * TOP // (2 * experts_all)
    slots = -(-capacity // 16) * 16
    core = me % 2

    held = {0: tokens}

    def tables_after(*earlier):
        own = after(slot_tables(expert_ids, gate_prob, experts_all), *earlier)
        every = lax.all_to_all(
            own.reshape(dp_count, experts, 2, rows), "dp", split_axis=0, concat_axis=0, tiled=True
        )
        return every[me ^ jnp.arange(dp_count, dtype=jnp.int32)]

    def tables_of(groups):
        order = [group | b for group in groups for b in (0, 2)]
        chosen = jnp.stack([held["tables"][r] for r in order + [r | 1 for r in order]])
        return chosen[:, :, 0].reshape(-1, rows), chosen[:, :, 1].reshape(-1, rows)

    def hidden_of(groups, *earlier):
        own = [held[group | q] for group in groups for q in range(4)]
        others = [held["c", group] for group in groups]
        return run_hidden(own, others, after(tables_of(groups)[0], *earlier), w_gate, w_up, slots)

    def outputs_of(groups, hidden, *earlier):
        pos, weight = tables_of(groups)
        mine, *others = run_outputs(hidden, after(pos, *earlier), weight, w_down, slots, half)
        return mine.reshape(-1, 4, rows, half), others

    sums, received = {}, {}

    def add_swapped(groups, mine, others, *earlier):
        for n, group in enumerate(groups):
            back = received["c", group] = hop(after(others[n], *earlier), "core")
            back = back.reshape(4, rows, half)
            for q in range(4):
                at = jnp.where(core == 0, q, (q % 2) * 2 + q // 2)
                sums[group | q] = [lax.dynamic_index_in_dim(v, at, 0, keepdims=False) for v in (mine[n], back)]

    def total(j):
        terms = sums[j] + [received[k] for k in SPREAD if k & ~BIT[HOP[k]] == j]
        return sum(t.astype(F32) for t in terms).astype(BF16)

    def spread_all(plan, *fence):
        for j, earlier in plan:
            earlier = [held[k] for k in earlier] + list(fence)
            if j == "tables":
                held[j] = tables_after(*earlier)
            elif isinstance(j, tuple):
                pieces = [after(held[j[1] | q], *earlier) if q else held[j[1]] for q in range(4)]
                held[j] = hop(jnp.stack(pieces), "core")
            else:
                held[j] = hop(after(held[j & ~BIT[HOP[j]]], *earlier), HOP[j])

    def collect_all(plan, *fence):
        for j, earlier in plan:
            earlier = [received[k] for k in earlier] + list(fence)
            received[j] = hop(after(total(j), *earlier), HOP[j])

    spread_all(SPREAD_AFTER)
    near = hidden_of((0, 4))
    spread_all([(("c", 8), ()), (("c", 12), ())], near)
    far = hidden_of((12, 8))
    mine, others = outputs_of((12, 8), far)
    add_swapped((12, 8), mine, others)
    mine, others = outputs_of((0, 4), near, received["c", 12])
    add_swapped((0, 4), mine, others)
    collect_all(COLLECT_AFTER)
    return total(0)


def on_device(tokens, expert_ids, gate_prob, w_gate, w_up, w_down):
    dp_count = lax.axis_size("dp")
    tok_rows = tokens.shape[0]
    local_experts = w_gate.shape[0]
    experts_all = local_experts * dp_count
    capacity = 3 * tok_rows * TOP // (2 * experts_all)
    flat_ids = expert_ids.reshape(-1)
    pair_count = flat_ids.shape[0]
    onehot = (flat_ids[:, None] == jnp.arange(experts_all, dtype=jnp.int32)[None, :]).astype(
        jnp.int32
    )
    before = jnp.cumsum(onehot, axis=0, dtype=jnp.int32) - onehot
    slot_pos = jnp.sum(before * onehot, axis=1, dtype=jnp.int32)
    flat_slot = flat_ids * capacity + slot_pos
    owner_row = jnp.arange(pair_count, dtype=jnp.int32) // TOP
    source_row = (
        jnp.full((experts_all * capacity,), tok_rows, jnp.int32).at[flat_slot].set(owner_row)
    )
    weights = gate_prob.reshape(-1)
    gathered = lax.all_gather(tokens, "expert", axis=1, tiled=True)
    padded = jnp.concatenate([gathered, jnp.zeros((1, gathered.shape[1]), gathered.dtype)], axis=0)
    arrived = lax.all_to_all(
        padded[source_row].reshape(dp_count, local_experts, capacity, gathered.shape[1]),
        "dp",
        split_axis=0,
        concat_axis=0,
        tiled=True,
    )
    gate_sum = jnp.einsum("sqcd,qfd->sqcf", arrived, w_gate, preferred_element_type=jnp.float32)
    up_sum = jnp.einsum("sqcd,qfd->sqcf", arrived, w_up, preferred_element_type=jnp.float32)
    hidden = (jax.nn.silu(gate_sum) * up_sum).astype(jnp.bfloat16)
    partial_value = jnp.einsum("sqcf,qfd->sqcd", hidden, w_down, preferred_element_type=jnp.float32)
    partial_value = partial_value.astype(jnp.bfloat16)
    returned = lax.all_to_all(partial_value, "dp", split_axis=0, concat_axis=0, tiled=True)
    flat_rows = returned.reshape(experts_all * capacity, returned.shape[3])
    picked = flat_rows[flat_slot].astype(jnp.float32)
    scaled = picked * weights[:, None]
    return lax.psum_scatter(
        jnp.sum(scaled.reshape(tok_rows, TOP, returned.shape[3]), axis=1).astype(jnp.bfloat16),
        "expert",
        scatter_dimension=1,
        tiled=True,
    )


def solution(mesh):
    in_specs = (
        P("dp", "expert"),
        P("dp", None),
        P("dp", None),
        P("dp", "expert", None),
        P("dp", "expert", None),
        P("dp", "expert", None),
    )
    out_specs = P("dp", "expert")
    plan = on_block if (mesh.shape["dp"], mesh.shape["expert"]) == (16, 2) else on_device
    return jax.shard_map(plan, mesh=mesh, in_specs=in_specs, out_specs=out_specs, check_vma=False)
```
